32 devices in a mesh: lev: 4 (over z), mem: 8 (over y, x, core).
Axes of the slice: x: 2, y: 2, z: 4, core: 2. Of those that a mesh axis runs over, the one named last changes fastest.
Arguments:
- perturbations: bfloat16 [32, 2, 64, 256, 256], P('mem', None, 'lev'), may hold values from -6 to 6
- gradient: bfloat16 [2, 64, 256, 256], P(None, 'lev', 'mem'), may hold values from -6 to 6
- member_scale: int32 [32], P('mem'), may hold values from 0 to 3
- kernel_y: bfloat16 [4, 256, 256], replicated, may hold values from 0 to 1, as said below
- kernel_x: bfloat16 [4, 256, 256], replicated, may hold values from 0 to 1, as said below
- vertical_weights: float32 [4, 5], replicated, may hold values from 0.2 to 1
- layer_index: int32 [64], replicated, may hold values from 0 to 7, never falling along the last dimension, each value on 1 to 16 neighbouring positions
Outputs:
- increment: float32 [2, 64, 256, 256], P(None, 'lev', 'mem')
The draws below stay inside these ranges and needn't reach their ends.
Inputs may be any that keep to these rules, and one draw needn't show every extreme that they name: `layer_index`: layer numbers never fall from one level to the next; every layer has at least one level and at most 16. `kernel_y`: each scale's matrix has nonnegative entries and rows that sum to one. `kernel_x`: each scale's matrix has nonnegative entries and rows that sum to one.
All inputs are finite; a program needn't handle non-finite values.
Results may differ from the reference program's by a relative error of at most 0.0039.
Values may be sent and summed in bfloat16 or wider, within the bound.
A program may use at most 128 MiB of HBM per device.

```python
import math
import jax
import jax.numpy as jnp
import numpy as np
from jax import lax

NY = 256
NX = 256
SCALES = 4
LEVELS = 64
MEMBERS = 32


def kernel_table(key, width):
    places = jnp.arange(width, dtype=jnp.float32)
    distance = jnp.abs(places[:, None] - places[None, :])
    length = 1.5 * 3.0 ** jnp.arange(SCALES, dtype=jnp.float32)
    rough = jax.random.uniform(key, (SCALES, width, width), jnp.float32, 0.5, 1.5)
    table = jnp.exp(-distance[None] / length[:, None, None]) * rough
    return (table / jnp.sum(table, axis=2, keepdims=True)).astype(jnp.bfloat16)


def draw_kernel_y(key, part):
    return kernel_table(jax.random.fold_in(key, 11), NY)


def draw_kernel_x(key, part):
    return kernel_table(jax.random.fold_in(key, 23), NX)


def touch_ends(result, own_key, least, largest):
    longest = result.shape.index(max(result.shape))
    spots = []
    for shift in (0, 1):
        where = [jax.random.randint(jax.random.fold_in(own_key, axis), (), 0, length) for axis, length in enumerate(result.shape)]
        where[longest] = (where[longest] + shift) % result.shape[longest]
        spots.append(tuple(where))
    return result.at[spots[0]].set(least).at[spots[1]].set(largest)


def spiked(entries, own_key, source, target, shards_of, factor):
    def block_of(axis_at):
        return (jnp.arange(entries.shape[axis_at]) // (entries.shape[axis_at] // shards_of)).reshape((-1,) + (1,) * (entries.ndim - 1 - axis_at))

    first = jax.random.permutation(own_key, shards_of)[block_of(target)]
    second = (block_of(target) + shards_of // 2) % shards_of
    return jnp.where((block_of(source) == first) | (block_of(source) == second), factor * entries, entries)


def block_scale(own_key, extent, split, low, largest):
    def one(axis_at, parts):
        draws = jax.random.uniform(jax.random.fold_in(jax.random.fold_in(own_key, 6), axis_at), (parts,), jnp.float32, low / len(split), largest / len(split))
        return jnp.repeat(jnp.exp(draws), extent[axis_at] // parts).reshape((-1,) + (1,) * (len(extent) - axis_at - 1))

    gain = one(*split[0])
    for cut in split[1:]:
        gain = gain * one(*cut)
    return gain


def profile(amount, total, bound, lean):
    loads = [(1 << 20) // math.isqrt(standing ** lean) + 1 for standing in range(2, amount + 1)]
    rest, counts = total - bound - (amount - 1), [1] * (amount - 1)
    while rest > 0:
        candidates = [i for i in range(amount - 1) if counts[i] < bound]
        mass, remaining = sum([loads[i] for i in candidates]), rest
        for i in candidates:
            more = min(bound - counts[i], max(1, remaining * loads[i] // mass), rest)
            counts[i] = counts[i] + more
            rest = rest - more
    return np.array([bound] + counts)


def ragged(key, count, total, most, lean):
    if count == 2:
        one = jax.random.randint(key, (), max(1, total - most), min(most, total - 1) + 1)
        return jnp.stack([one, total - one])
    tallies = jnp.asarray(profile(count, total, most, lean), jnp.int32)
    couples = (count - 1) // 2
    source_of, sink = tallies[1:1 + 2 * couples:2], tallies[2:2 + 2 * couples:2]
    slack = jnp.minimum(source_of - 1, most - sink)
    passed = jax.random.randint(jax.random.fold_in(key, 1), (couples,), 0, 1 << 20) % (slack + 1)
    tallies = tallies.at[1:1 + 2 * couples:2].set(source_of - passed).at[2:2 + 2 * couples:2].set(sink + passed)
    return tallies[jax.random.permutation(jax.random.fold_in(key, 2), count)]


def scatter_about(key, dims, scale, most, pieces=(), kind=jnp.bfloat16):
    result = scale * jax.random.normal(key, dims, jnp.float32)
    if pieces:
        result = result * block_scale(key, dims, pieces, -0.22, 0.18)
    return jnp.clip(result, -most, most).astype(kind)


def bell_draw_with(rng, extent, spread, reach, cuts, heavy, held_as=jnp.bfloat16):
    result = spread * jax.random.normal(rng, extent, jnp.float32)
    if cuts:
        result = result * block_scale(rng, extent, cuts, -0.22, 0.18)
    return jnp.clip(spiked(result, jax.random.fold_in(rng, 3), *heavy), -reach, reach).astype(held_as)


def setup_inputs(seed: int = 0) -> dict:
    key_list = jax.random.split(jax.random.key(seed), 8)
    return {
        "perturbations": bell_draw_with(key_list[0], (MEMBERS, 2, LEVELS, NY, NX), 1.0, 6.0, ((0, 8), (2, 4)), (0, 3, 8, 2.0)),
        "gradient": scatter_about(key_list[1], (2, LEVELS, NY, NX), 1.0, 6.0, ((1, 4), (2, 8))),
        "member_scale": touch_ends(jax.random.randint(key_list[2], (MEMBERS,), 0, SCALES), jax.random.fold_in(key_list[2], 1), 0, SCALES - 1).astype(jnp.int32),
        "kernel_y": draw_kernel_y(jax.random.fold_in(key_list[7], 71), 0),
        "kernel_x": draw_kernel_x(jax.random.fold_in(key_list[7], 71), 0),
        "vertical_weights": jnp.clip(jax.random.uniform(key_list[5], (SCALES, 5), jnp.float32, 0.2, 1.0), 0.2, 1.0),
        "layer_index": jnp.searchsorted(jnp.cumsum(ragged(key_list[6], max(3, LEVELS // 8), LEVELS, min(16, LEVELS // 2), 0)), jnp.arange(LEVELS), side="right").astype(jnp.int32),
    }


def reference(perturbations, gradient, member_scale, kernel_y, kernel_x, vertical_weights, layer_index):
    levels = perturbations.shape[2]
    grad_full = gradient.astype(jnp.float32)
    padded_ids = jnp.pad(layer_index, 2, constant_values=-1)

    def step(total, inputs):
        member, scale = inputs
        product = (member.astype(jnp.float32) * grad_full).astype(jnp.bfloat16)
        rows_k = jnp.einsum("ij,vljx->vlix", kernel_y[scale].astype(jnp.float32), product.astype(jnp.float32), precision=lax.Precision.HIGHEST).astype(jnp.bfloat16)
        horizontal = jnp.einsum("vlib,ab->vlia", rows_k.astype(jnp.float32), kernel_x[scale].astype(jnp.float32), precision=lax.Precision.HIGHEST).astype(jnp.bfloat16)
        padded = jnp.pad(horizontal.astype(jnp.float32), ((0, 0), (2, 2), (0, 0), (0, 0)))
        mixed = jnp.zeros(horizontal.shape, jnp.float32)
        for offset in range(-2, 3):
            same = (padded_ids[2 + offset:2 + offset + levels] == layer_index).astype(jnp.float32)
            mixed = mixed + vertical_weights[scale, offset + 2] * same[None, :, None, None] * padded[:, 2 + offset:2 + offset + levels]
        return total + member.astype(jnp.float32) * mixed, None

    total, _ = lax.scan(step, jnp.zeros(gradient.shape, jnp.float32), (perturbations, member_scale))
    return total / (perturbations.shape[0] - 1)
```

```python
import functools

import jax
import jax.numpy as jnp
from jax import lax
from jax.experimental import pallas as pl
from jax.experimental.pallas import tpu as pltpu
from jax.sharding import PartitionSpec as P

MESH = pl.DeviceIdType.MESH
REACH = 2
SPAN = 2 * REACH + 1
WIDE = 2
SUB = 16


def kernel(
    n_lev, n_mem,
    scale_ref, weights_ref, layer_ref, pert_hbm, grad_hbm, ky_hbm, kx_hbm,
    out_ref,
    pbuf, gbuf, hbuf, part, near, far, ky, kx, kxt, wtab,
    p_sem, g_sem, t_sem, ag_send, ag_fwd, ag_recv, z_send, z_recv,
    r1_send, r1_recv, r2_send, r2_recv,
):
    count, var, levels, ny, nx = pert_hbm.shape
    rows = grad_hbm.shape[2]
    chips = n_mem // 2
    chunks = levels // WIDE
    lev = lax.axis_index("lev")
    mem = lax.axis_index("mem")
    chip = mem // 2
    core = mem % 2
    other = 1 - core
    sibling = chip * 2 + other
    has_low = lev > 0
    has_high = lev < n_lev - 1
    last = chunks - 1

    def chip_at(step):
        return lax.rem(chip + step, chips)

    def order(t):
        return 0 if t == 0 else (last if t == 1 else t - 1)

    def pert_copy(j):
        at = pl.ds(j * WIDE, WIDE)
        return pltpu.make_async_copy(pert_hbm.at[:, :, at], pbuf.at[:, :, at], p_sem.at[j])

    own_rows = pl.ds(pl.multiple_of(mem * rows, rows), rows)
    grad_copy = pltpu.make_async_copy(grad_hbm, gbuf.at[:, :, own_rows], g_sem)
    ky_copy = pltpu.make_async_copy(ky_hbm, ky, t_sem.at[0])
    kx_copy = pltpu.make_async_copy(kx_hbm, kx, t_sem.at[1])

    barrier = pltpu.get_barrier_semaphore()
    for step in range(1, chips):
        pl.semaphore_signal(
            barrier, inc=1, device_id=(lev, chip_at(step) * 2 + core), device_id_type=MESH
        )
    pl.semaphore_signal(barrier, inc=1, device_id=(lev, sibling), device_id_type=MESH)

    @pl.when(has_low)
    def _():
        pl.semaphore_signal(barrier, inc=1, device_id=(lev - 1, mem), device_id_type=MESH)

    @pl.when(has_high)
    def _():
        pl.semaphore_signal(barrier, inc=1, device_id=(lev + 1, mem), device_id_type=MESH)

    grad_copy.start()
    kx_copy.start()
    ky_copy.start()
    for t in range(chunks):
        pert_copy(order(t)).start()
    pl.semaphore_wait(barrier, chips + (lev > 0).astype(jnp.int32) + (lev < n_lev - 1).astype(jnp.int32))

    def gather_send(j, target, send_sem):
        at = pl.ds(j * WIDE, WIDE)
        return pltpu.make_async_remote_copy(
            src_ref=grad_hbm.at[:, at],
            dst_ref=gbuf.at[:, at, own_rows],
            send_sem=send_sem,
            recv_sem=ag_recv.at[j, mem],
            device_id=(lev, target),
            device_id_type=MESH,
        )

    def gather_sends(j):
        pairs = [(chip_at(step) * 2 + core, ag_send.at[j, chip_at(step)]) for step in range(1, chips)]
        return [gather_send(j, *pair) for pair in pairs + [(sibling, ag_send.at[j, chip])]]

    def block_move(j, source):
        at = pl.ds(j * WIDE, WIDE)
        place = gbuf.at[:, at, pl.ds(pl.multiple_of(source * rows, rows), rows)]
        return pltpu.make_async_remote_copy(
            src_ref=place,
            dst_ref=place,
            send_sem=ag_fwd.at[j, source // 2],
            recv_sem=ag_recv.at[j, source],
            device_id=(lev, sibling),
            device_id_type=MESH,
        )

    for t in range(chunks):
        for copy in gather_sends(order(t)):
            copy.start()

    def forward(j):
        for step in range(1, chips):
            move = block_move(j, chip_at(step) * 2 + core)
            move.wait_recv()
            move.start()

    def ready(j):
        block_move(j, sibling).wait_recv()
        for step in range(1, chips):
            block_move(j, chip_at(step) * 2 + other).wait_recv()

    def weight_row(l, _):
        here = lev * levels + l
        own = layer_ref[here]
        for d in range(SPAN):
            there = here + d - REACH
            inside = (there >= 0) & (there < levels * n_lev)
            same = inside & (layer_ref[jnp.clip(there, 0, levels * n_lev - 1)] == own)
            for k in range(count):
                wtab[l, k * SPAN + d] = jnp.where(same, weights_ref[scale_ref[k], d], 0.0)
        return 0

    lax.fori_loop(0, levels, weight_row, 0)

    @pl.when(lev == 0)
    def _():
        hbuf[:, :, pl.ds(0, REACH)] = jnp.zeros((count, var, REACH, ny, nx), jnp.bfloat16)

    @pl.when(lev == n_lev - 1)
    def _():
        hbuf[:, :, pl.ds(REACH + levels, REACH)] = jnp.zeros((count, var, REACH, ny, nx), jnp.bfloat16)

    kx_copy.wait()
    for k in range(count):
        kxt[k] = kx[scale_ref[k]].T
    ky_copy.wait()

    def halo_move(side, k):
        source = REACH if side == 0 else levels
        place = levels + REACH if side == 0 else 0
        return pltpu.make_async_remote_copy(
            src_ref=hbuf.at[k, :, pl.ds(source, REACH)],
            dst_ref=hbuf.at[k, :, pl.ds(place, REACH)],
            send_sem=z_send.at[side, k],
            recv_sem=z_recv.at[side, k],
            device_id=(lev - 1 if side == 0 else lev + 1, mem),
            device_id_type=MESH,
        )

    def smooth(j, side=None):
        def member(k, _):
            kyk = ky[scale_ref[k]]
            kxk = kxt[k]
            for v in range(var):
                for l in range(WIDE):
                    at = j * WIDE + l
                    product = pbuf[k, v, at] * gbuf[v, at]
                    summed = jnp.dot(kyk, product, preferred_element_type=jnp.float32)
                    done = jnp.dot(
                        summed.astype(jnp.bfloat16), kxk, preferred_element_type=jnp.float32
                    )
                    hbuf[k, v, REACH + at] = done.astype(jnp.bfloat16)
            if side is not None:

                @pl.when(has_low if side == 0 else has_high)
                def _():
                    halo_move(side, k).start()

            return 0

        lax.fori_loop(0, count, member, 0)

    def mix(j):
        def block(i, _):
            v = i // n_mem
            target = i % n_mem
            for b in range(rows // SUB):
                at = pl.ds(pl.multiple_of(target * rows + b * SUB, SUB), SUB)
                total = [jnp.zeros((SUB, nx), jnp.float32) for _ in range(WIDE)]
                for k in range(count):
                    near_levels = [
                        hbuf[k, v, j * WIDE + e, at].astype(jnp.float32)
                        for e in range(WIDE + 2 * REACH)
                    ]
                    for l in range(WIDE):
                        mixed = wtab[j * WIDE + l, k * SPAN] * near_levels[l]
                        for d in range(1, SPAN):
                            mixed = mixed + wtab[j * WIDE + l, k * SPAN + d] * near_levels[l + d]
                        total[l] = total[l] + pbuf[k, v, j * WIDE + l, at].astype(jnp.float32) * mixed
                for l in range(WIDE):
                    part[j, target % 2, target // 2, v, l, pl.ds(b * SUB, SUB)] = total[l].astype(
                        jnp.bfloat16
                    )
            return 0

        lax.fori_loop(0, var * n_mem, block, 0)

    def near_move(j):
        return pltpu.make_async_remote_copy(
            src_ref=part.at[j, other],
            dst_ref=near.at[j],
            send_sem=r1_send.at[j],
            recv_sem=r1_recv.at[j],
            device_id=(lev, sibling),
            device_id_type=MESH,
        )

    def far_move(j, place, slot):
        return pltpu.make_async_remote_copy(
            src_ref=part.at[j, core, place],
            dst_ref=far.at[slot, j],
            send_sem=r2_send.at[j, place],
            recv_sem=r2_recv.at[j, slot],
            device_id=(lev, place * 2 + core),
            device_id_type=MESH,
        )

    def pass_on(j):
        near_move(j).wait_recv()
        for step in range(1, chips):
            place = chip_at(step)
            both = part[j, core, place].astype(jnp.float32) + near[j, place].astype(jnp.float32)
            part[j, core, place] = both.astype(jnp.bfloat16)
            far_move(j, place, chip).start()

    def finish(j):
        total = part[j, core, chip].astype(jnp.float32) + near[j, chip].astype(jnp.float32)
        for step in range(1, chips):
            place = chip_at(step)
            far_move(j, place, place).wait_recv()
            total = total + far[place, j].astype(jnp.float32)
        out_ref[:, pl.ds(j * WIDE, WIDE)] = total * (1.0 / (count * n_mem - 1))

    def work(j, side=None):
        ready(j)
        pert_copy(j).wait()
        smooth(j, side)

    forward(0)
    forward(last)
    grad_copy.wait()
    work(0, 0)
    forward(1)
    work(last, 1)
    forward(2)
    work(1)

    def steady(j, _):
        @pl.when(j < last - 1)
        def _():
            forward(j + 1)

        work(j)
        mix(j - 1)
        near_move(j - 1).start()

        @pl.when(j > 2)
        def _():
            pass_on(j - 2)

        return 0

    lax.fori_loop(2, last, steady, 0)
    mix(last - 1)
    near_move(last - 1).start()
    pass_on(last - 2)
    pass_on(last - 1)

    def early(j, _):
        finish(j)
        return 0

    lax.fori_loop(1, last - 1, early, 0)

    def halo_wait(side):
        @pl.when(has_high if side == 0 else has_low)
        def _():
            for k in range(count):
                halo_move(side, k).wait_recv()

    halo_wait(1)
    mix(0)
    near_move(0).start()
    halo_wait(0)
    mix(last)
    near_move(last).start()
    pass_on(0)
    pass_on(last)
    finish(last - 1)
    finish(0)
    finish(last)

    def drain(j, _):
        for copy in gather_sends(j):
            copy.wait_send()
        near_move(j).wait_send()
        for step in range(1, chips):
            block_move(j, chip_at(step) * 2 + core).wait_send()
            far_move(j, chip_at(step), chip).wait_send()
        return 0

    lax.fori_loop(0, chunks, drain, 0)
    for side in range(2):

        @pl.when(has_low if side == 0 else has_high)
        def _(side=side):
            for k in range(count):
                halo_move(side, k).wait_send()


def per_device(
    n_lev, n_mem,
    perturbations, gradient, member_scale, kernel_y, kernel_x, vertical_weights, layer_index,
):
    count, var, levels, ny, nx = perturbations.shape
    rows = gradient.shape[2]
    chips = n_mem // 2
    chunks = levels // WIDE
    half = jnp.bfloat16
    dma = pltpu.SemaphoreType.DMA
    smem = pl.BlockSpec(memory_space=pltpu.SMEM)
    anywhere = pl.BlockSpec(memory_space=pl.ANY)
    units = count * var * levels
    return pl.pallas_call(
        functools.partial(kernel, n_lev, n_mem),
        out_shape=jax.ShapeDtypeStruct(gradient.shape, jnp.float32),
        in_specs=[smem, smem, smem, anywhere, anywhere, anywhere, anywhere],
        out_specs=pl.BlockSpec(memory_space=pltpu.VMEM),
        scratch_shapes=[
            pltpu.VMEM(perturbations.shape, half),
            pltpu.VMEM((var, levels, ny, nx), half),
            pltpu.VMEM((count, var, levels + 2 * REACH, ny, nx), half),
            pltpu.VMEM((chunks, 2, chips, var, WIDE, rows, nx), half),
            pltpu.VMEM((chunks, chips, var, WIDE, rows, nx), half),
            pltpu.VMEM((chips, chunks, var, WIDE, rows, nx), half),
            pltpu.VMEM(kernel_y.shape, half),
            pltpu.VMEM(kernel_x.shape, half),
            pltpu.VMEM((count, nx, nx), half),
            pltpu.SMEM((levels, count * SPAN), jnp.float32),
            dma((chunks,)),
            dma,
            dma((2,)),
            dma((chunks, chips)),
            dma((chunks, chips)),
            dma((chunks, n_mem)),
            dma((2, count)),
            dma((2, count)),
            dma((chunks,)),
            dma((chunks,)),
            dma((chunks, chips)),
            dma((chunks, chips)),
        ],
        compiler_params=pltpu.CompilerParams(
            collective_id=0, has_side_effects=True, vmem_limit_bytes=60 * 2**20
        ),
        cost_estimate=pl.CostEstimate(
            flops=units * 2 * ny * nx * (ny + nx),
            bytes_accessed=perturbations.size * 2,
            transcendentals=0,
        ),
    )(
        member_scale, vertical_weights, layer_index,
        perturbations, gradient, kernel_y, kernel_x,
    )


def solution(mesh):
    placed = (
        P("mem", None, "lev", None, None),
        P(None, "lev", "mem", None),
        P("mem"),
        P(),
        P(),
        P(),
        P(),
    )
    return jax.shard_map(
        functools.partial(per_device, mesh.shape["lev"], mesh.shape["mem"]),
        mesh=mesh,
        in_specs=placed,
        out_specs=P(None, "lev", "mem", None),
        check_vma=False,
    )
```

```python
import functools

import jax
import jax.numpy as jnp
from jax import lax
from jax.experimental import pallas as pl
from jax.experimental.pallas import tpu as pltpu
from jax.sharding import PartitionSpec as P

MESH = pl.DeviceIdType.MESH
REACH = 2
SPAN = 2 * REACH + 1
WIDE = 2
SUB = 16


def kernel(
    n_lev, n_mem,
    scale_ref, weights_ref, layer_ref, pert_hbm, grad_hbm, ky_hbm, kx_hbm,
    out_ref,
    pbuf, gbuf, hbuf, part, near, far, ky, kx, kxt, wtab,
    p_sem, g_sem, t_sem, ag_send, ag_fwd, ag_recv, z_send, z_recv,
    r1_send, r1_recv, r2_send, r2_recv,
):
    count, var, levels, ny, nx = pert_hbm.shape
    rows = grad_hbm.shape[2]
    chips = n_mem // 2
    chunks = levels // WIDE
    lev = lax.axis_index("lev")
    mem = lax.axis_index("mem")
    chip = mem // 2
    core = mem % 2
    other = 1 - core
    sibling = chip * 2 + other
    has_low = lev > 0
    has_high = lev < n_lev - 1
    last = chunks - 1

    def chip_at(step):
        return lax.rem(chip + step, chips)

    def order(t):
        return 0 if t == 0 else (last if t == 1 else t - 1)

    def pert_copy(j):
        at = pl.ds(j * WIDE, WIDE)
        return pltpu.make_async_copy(pert_hbm.at[:, :, at], pbuf.at[:, :, at], p_sem.at[j])

    own_rows = pl.ds(pl.multiple_of(mem * rows, rows), rows)
    grad_copy = pltpu.make_async_copy(grad_hbm, gbuf.at[:, :, own_rows], g_sem)
    ky_copy = pltpu.make_async_copy(ky_hbm, ky, t_sem.at[0])
    kx_copy = pltpu.make_async_copy(kx_hbm, kx, t_sem.at[1])

    barrier = pltpu.get_barrier_semaphore()
    for step in range(1, chips):
        pl.semaphore_signal(
            barrier, inc=1, device_id=(lev, chip_at(step) * 2 + core), device_id_type=MESH
        )
    pl.semaphore_signal(barrier, inc=1, device_id=(lev, sibling), device_id_type=MESH)

    @pl.when(has_low)
    def _():
        pl.semaphore_signal(barrier, inc=1, device_id=(lev - 1, mem), device_id_type=MESH)

    @pl.when(has_high)
    def _():
        pl.semaphore_signal(barrier, inc=1, device_id=(lev + 1, mem), device_id_type=MESH)

    grad_copy.start()
    kx_copy.start()
    ky_copy.start()
    for t in range(chunks):
        pert_copy(order(t)).start()
    pl.semaphore_wait(barrier, chips + (lev > 0).astype(jnp.int32) + (lev < n_lev - 1).astype(jnp.int32))

    def gather_send(j, target, send_sem):
        at = pl.ds(j * WIDE, WIDE)
        return pltpu.make_async_remote_copy(
            src_ref=grad_hbm.at[:, at],
            dst_ref=gbuf.at[:, at, own_rows],
            send_sem=send_sem,
            recv_sem=ag_recv.at[j, mem],
            device_id=(lev, target),
            device_id_type=MESH,
        )

    def gather_sends(j):
        pairs = [(chip_at(step) * 2 + core, ag_send.at[j, chip_at(step)]) for step in range(1, chips)]
        return [gather_send(j, *pair) for pair in pairs + [(sibling, ag_send.at[j, chip])]]

    def block_move(j, source):
        at = pl.ds(j * WIDE, WIDE)
        place = gbuf.at[:, at, pl.ds(pl.multiple_of(source * rows, rows), rows)]
        return pltpu.make_async_remote_copy(
            src_ref=place,
            dst_ref=place,
            send_sem=ag_fwd.at[j, source // 2],
            recv_sem=ag_recv.at[j, source],
            device_id=(lev, sibling),
            device_id_type=MESH,
        )

    for t in range(chunks):
        for copy in gather_sends(order(t)):
            copy.start()

    def forward(j):
        for step in range(1, chips):
            move = block_move(j, chip_at(step) * 2 + core)
            move.wait_recv()
            move.start()

    def ready(j):
        block_move(j, sibling).wait_recv()
        for step in range(1, chips):
            block_move(j, chip_at(step) * 2 + other).wait_recv()

    def weight_row(l, _):
        here = lev * levels + l
        own = layer_ref[here]
        for d in range(SPAN):
            there = here + d - REACH
            inside = (there >= 0) & (there < levels * n_lev)
            same = inside & (layer_ref[jnp.clip(there, 0, levels * n_lev - 1)] == own)
            for k in range(count):
                wtab[l, k * SPAN + d] = jnp.where(same, weights_ref[scale_ref[k], d], 0.0)
        return 0

    @pl.when(lev == 0)
    def _():
        hbuf[:, :, pl.ds(0, REACH)] = jnp.zeros((count, var, REACH, ny, nx), jnp.bfloat16)

    @pl.when(lev == n_lev - 1)
    def _():
        hbuf[:, :, pl.ds(REACH + levels, REACH)] = jnp.zeros((count, var, REACH, ny, nx), jnp.bfloat16)

    kx_copy.wait()
    for k in range(count):
        kxt[k] = kx[scale_ref[k]].T
    ky_copy.wait()

    def halo_move(side, k):
        source = REACH if side == 0 else levels
        place = levels + REACH if side == 0 else 0
        return pltpu.make_async_remote_copy(
            src_ref=hbuf.at[k, :, pl.ds(source, REACH)],
            dst_ref=hbuf.at[k, :, pl.ds(place, REACH)],
            send_sem=z_send.at[side, k],
            recv_sem=z_recv.at[side, k],
            device_id=(lev - 1 if side == 0 else lev + 1, mem),
            device_id_type=MESH,
        )

    def smooth(j, side=None):
        def member(k, _):
            kyk = ky[scale_ref[k]]
            kxk = kxt[k]
            for v in range(var):
                for l in range(WIDE):
                    at = j * WIDE + l
                    product = pbuf[k, v, at] * gbuf[v, at]
                    summed = jnp.dot(kyk, product, preferred_element_type=jnp.float32)
                    done = jnp.dot(
                        summed.astype(jnp.bfloat16), kxk, preferred_element_type=jnp.float32
                    )
                    hbuf[k, v, REACH + at] = done.astype(jnp.bfloat16)
            if side is not None:

                @pl.when(has_low if side == 0 else has_high)
                def _():
                    halo_move(side, k).start()

            return 0

        lax.fori_loop(0, count, member, 0)

    def mix(j):
        def block(i, _):
            v = i // n_mem
            target = i % n_mem
            for b in range(rows // SUB):
                at = pl.ds(pl.multiple_of(target * rows + b * SUB, SUB), SUB)
                total = [jnp.zeros((SUB, nx), jnp.float32) for _ in range(WIDE)]
                for k in range(count):
                    near_levels = [
                        hbuf[k, v, j * WIDE + e, at].astype(jnp.float32)
                        for e in range(WIDE + 2 * REACH)
                    ]
                    for l in range(WIDE):
                        mixed = wtab[j * WIDE + l, k * SPAN] * near_levels[l]
                        for d in range(1, SPAN):
                            mixed = mixed + wtab[j * WIDE + l, k * SPAN + d] * near_levels[l + d]
                        total[l] = total[l] + pbuf[k, v, j * WIDE + l, at].astype(jnp.float32) * mixed
                for l in range(WIDE):
                    part[j, target % 2, target // 2, v, l, pl.ds(b * SUB, SUB)] = total[l].astype(
                        jnp.bfloat16
                    )
            return 0

        lax.fori_loop(0, var * n_mem, block, 0, unroll=2)

    def near_move(j):
        return pltpu.make_async_remote_copy(
            src_ref=part.at[j, other],
            dst_ref=near.at[j],
            send_sem=r1_send.at[j],
            recv_sem=r1_recv.at[j],
            device_id=(lev, sibling),
            device_id_type=MESH,
        )

    def far_move(j, place, slot):
        return pltpu.make_async_remote_copy(
            src_ref=part.at[j, core, place],
            dst_ref=far.at[slot, j],
            send_sem=r2_send.at[j, place],
            recv_sem=r2_recv.at[j, slot],
            device_id=(lev, place * 2 + core),
            device_id_type=MESH,
        )

    def pass_on(j):
        near_move(j).wait_recv()
        for step in range(1, chips):
            place = chip_at(step)
            both = part[j, core, place].astype(jnp.float32) + near[j, place].astype(jnp.float32)
            part[j, core, place] = both.astype(jnp.bfloat16)
            far_move(j, place, chip).start()

    def finish(j):
        total = part[j, core, chip].astype(jnp.float32) + near[j, chip].astype(jnp.float32)
        for step in range(1, chips):
            place = chip_at(step)
            far_move(j, place, place).wait_recv()
            total = total + far[place, j].astype(jnp.float32)
        out_ref[:, pl.ds(j * WIDE, WIDE)] = total * (1.0 / (count * n_mem - 1))

    def work(j, side=None):
        ready(j)
        pert_copy(j).wait()
        smooth(j, side)

    forward(0)
    forward(last)
    grad_copy.wait()
    work(0, 0)
    forward(1)
    work(last, 1)
    forward(2)
    work(1)

    lax.fori_loop(0, levels, weight_row, 0)

    def steady(j, _):
        @pl.when(j < last - 1)
        def _():
            forward(j + 1)

        work(j)
        mix(j - 1)
        near_move(j - 1).start()

        @pl.when(j > 2)
        def _():
            pass_on(j - 2)

        return 0

    lax.fori_loop(2, last, steady, 0)
    mix(last - 1)
    near_move(last - 1).start()
    pass_on(last - 2)
    pass_on(last - 1)

    def halo_wait(side):
        @pl.when(has_high if side == 0 else has_low)
        def _():
            for k in range(count):
                halo_move(side, k).wait_recv()

    halo_wait(1)
    mix(0)
    near_move(0).start()
    halo_wait(0)
    pass_on(0)
    mix(last)
    near_move(last).start()
    pass_on(last)
    def early(j, _):
        finish(j)
        return 0

    lax.fori_loop(1, last - 1, early, 0)
    finish(last - 1)
    finish(0)
    finish(last)

    def drain(j, _):
        for copy in gather_sends(j):
            copy.wait_send()
        near_move(j).wait_send()
        for step in range(1, chips):
            block_move(j, chip_at(step) * 2 + core).wait_send()
            far_move(j, chip_at(step), chip).wait_send()
        return 0

    lax.fori_loop(0, chunks, drain, 0)
    for side in range(2):

        @pl.when(has_low if side == 0 else has_high)
        def _(side=side):
            for k in range(count):
                halo_move(side, k).wait_send()


def per_device(
    n_lev, n_mem,
    perturbations, gradient, member_scale, kernel_y, kernel_x, vertical_weights, layer_index,
):
    count, var, levels, ny, nx = perturbations.shape
    rows = gradient.shape[2]
    chips = n_mem // 2
    chunks = levels // WIDE
    half = jnp.bfloat16
    dma = pltpu.SemaphoreType.DMA
    smem = pl.BlockSpec(memory_space=pltpu.SMEM)
    anywhere = pl.BlockSpec(memory_space=pl.ANY)
    units = count * var * levels
    return pl.pallas_call(
        functools.partial(kernel, n_lev, n_mem),
        out_shape=jax.ShapeDtypeStruct(gradient.shape, jnp.float32),
        in_specs=[smem, smem, smem, anywhere, anywhere, anywhere, anywhere],
        out_specs=pl.BlockSpec(memory_space=pltpu.VMEM),
        scratch_shapes=[
            pltpu.VMEM(perturbations.shape, half),
            pltpu.VMEM((var, levels, ny, nx), half),
            pltpu.VMEM((count, var, levels + 2 * REACH, ny, nx), half),
            pltpu.VMEM((chunks, 2, chips, var, WIDE, rows, nx), half),
            pltpu.VMEM((chunks, chips, var, WIDE, rows, nx), half),
            pltpu.VMEM((chips, chunks, var, WIDE, rows, nx), half),
            pltpu.VMEM(kernel_y.shape, half),
            pltpu.VMEM(kernel_x.shape, half),
            pltpu.VMEM((count, nx, nx), half),
            pltpu.SMEM((levels, count * SPAN), jnp.float32),
            dma((chunks,)),
            dma,
            dma((2,)),
            dma((chunks, chips)),
            dma((chunks, chips)),
            dma((chunks, n_mem)),
            dma((2, count)),
            dma((2, count)),
            dma((chunks,)),
            dma((chunks,)),
            dma((chunks, chips)),
            dma((chunks, chips)),
        ],
        compiler_params=pltpu.CompilerParams(
            collective_id=0, has_side_effects=True, vmem_limit_bytes=60 * 2**20
        ),
        cost_estimate=pl.CostEstimate(
            flops=units * 2 * ny * nx * (ny + nx),
            bytes_accessed=perturbations.size * 2,
            transcendentals=0,
        ),
    )(
        member_scale, vertical_weights, layer_index,
        perturbations, gradient, kernel_y, kernel_x,
    )


def solution(mesh):
    placed = (
        P("mem", None, "lev", None, None),
        P(None, "lev", "mem", None),
        P("mem"),
        P(),
        P(),
        P(),
        P(),
    )
    return jax.shard_map(
        functools.partial(per_device, mesh.shape["lev"], mesh.shape["mem"]),
        mesh=mesh,
        in_specs=placed,
        out_specs=P(None, "lev", "mem", None),
        check_vma=False,
    )
```
